32 devices in a mesh: gx: 4 (over z), gy: 8 (over y, x, core).
Axes of the slice: x: 2, y: 2, z: 4, core: 2. Of those that a mesh axis runs over, the one named last changes fastest.
Arguments:
- misfit: bfloat16 [32, 32, 64, 128], P(('gx', 'gy')), may hold values from -6 to 6
- block_counts: int32 [32, 32], P(('gx', 'gy')), may hold values from 1 to 64, as said below
- slot_element: int32 [32, 32, 64], P(('gx', 'gy')), may hold values from 0 to 127
- observe: bfloat16 [128, 64], replicated, may hold values from -0.09375 to 0.09375
- stokes_blocks: bfloat16 [32, 128, 9, 64, 64], P('gx', 'gy'), may hold values from -0.25 to 0.25
- pattern: int32 [32, 128, 9], P('gx', 'gy'), may hold values 0 or 1
- velocity: bfloat16 [32, 128, 64], P('gx', 'gy'), may hold values from -6 to 6
- log_friction: float32 [32, 128], P('gx', 'gy'), may hold values from -1 to 1
Outputs:
- adjoint: float32 [32, 128, 64], P('gx', 'gy')
- gradient: float32 [32, 128], P('gx', 'gy')
The draws below stay inside these ranges and needn't reach their ends.
Inputs may be any that keep to these rules, and one draw needn't show every extreme that they name: `block_counts`: for every owner some source fills all 64 slots.
All inputs are finite; a program needn't handle non-finite values. No bound on the sum of `pattern` on one device may be relied on, other than what follows from the above.
Results may differ from the reference program's by a relative error of at most 0.0041.
Values may be sent and summed in bfloat16 or wider, within the bound.
A program may use at most 64 MiB of HBM per device.

```python
import jax
import jax.numpy as jnp
from jax import lax

D_OBS = 128
BLK = 64
EX = 8
EY = 16
CAP = 64
E_DEV = 128
NX = 32
NY = 128
N_GX = 4
N_GY = 8
DEVICES = 32


def draw_block_counts(key, part):
    first, second = jax.random.split(jax.random.fold_in(key, 11))
    counts = jax.random.randint(first, (DEVICES, DEVICES), 1, CAP + 1)
    fullest = jax.random.permutation(second, DEVICES)
    return jnp.where(jnp.arange(DEVICES)[None, :] == fullest[:, None], CAP, counts).astype(jnp.int32)


def plant(array, stream_key, smallest, largest):
    shape = array.shape
    place = [jax.random.randint(jax.random.fold_in(stream_key, axis), (), 0, shape[axis]) for axis in range(len(shape))]
    array = array.at[tuple(place)].set(smallest)
    longest = shape.index(max(shape))
    place[longest] = (place[longest] + 1) % shape[longest]
    return array.at[tuple(place)].set(largest)


def steps_of(key, dims, cuts, smallest, high):
    def one(dim, parts):
        heights = jax.random.uniform(jax.random.fold_in(jax.random.fold_in(key, 6), dim), (parts,), jnp.float32, smallest / len(cuts), high / len(cuts))
        return jnp.repeat(jnp.exp(heights), dims[dim] // parts).reshape((-1,) + (1,) * (len(dims) - dim - 1))

    level = one(*cuts[0])
    for cut in cuts[1:]:
        level = level * one(*cut)
    return level


def centred(stream_key, extent, deviation, reach, cuts=(), held_as=jnp.bfloat16):
    drawn = jax.random.normal(stream_key, extent, jnp.float32) * deviation
    if len(cuts) > 0:
        drawn = steps_of(stream_key, extent, cuts, -0.22, 0.18) * drawn
    return jnp.clip(drawn, min=-reach, max=reach).astype(held_as)


def setup_inputs(seed: int = 0) -> dict:
    splits = jax.random.split(jax.random.key(seed), 9)
    misfit = centred(splits[0], (DEVICES, DEVICES, CAP, D_OBS), 1.0, 6.0, ((0, 32),))
    block_counts = draw_block_counts(jax.random.fold_in(splits[8], 71), 0)
    slot_element = plant(jax.random.randint(splits[2], (DEVICES, DEVICES, CAP), 0, E_DEV), jax.random.fold_in(splits[2], 1), 0, E_DEV - 1).astype(jnp.int32)
    observe = centred(splits[3], (D_OBS, BLK), (D_OBS * 32) ** -0.5, 0.09375)
    stokes_blocks = centred(splits[4], (NX, NY, 9, BLK, BLK), (9 * BLK) ** -0.5, 0.25, ((0, 4), (1, 8)))
    pattern = plant((jax.random.randint(splits[5], (NX, NY, 9), 0, 4) < 3).astype(jnp.int32), jax.random.fold_in(splits[5], 1), 0, 1)
    velocity = centred(splits[6], (NX, NY, BLK), 1.0, 6.0, ((0, 4), (1, 8)))
    log_friction = jnp.clip(jax.random.uniform(splits[7], (NX, NY), jnp.float32, -1.0, 1.0) * steps_of(splits[7], (NX, NY), ((0, 4), (1, 8)), -0.4, 0.0), -1.0, 1.0)
    return {"misfit": misfit, "block_counts": block_counts, "slot_element": slot_element, "observe": observe, "stokes_blocks": stokes_blocks, "pattern": pattern, "velocity": velocity, "log_friction": log_friction}


def owner_forcing(args):
    blocks, counts, elems, observe = args[0], args[1], args[2], args[3]
    flat = blocks.reshape(DEVICES * CAP, D_OBS)
    projected = jnp.dot(flat, observe, preferred_element_type=jnp.float32).astype(jnp.bfloat16)
    live = jnp.arange(CAP)[None, :] < counts[:, None]
    onehot = ((elems[:, :, None] == jnp.arange(E_DEV)[None, None, :]) & live[:, :, None]).astype(jnp.bfloat16)
    onehot = onehot.reshape(DEVICES * CAP, E_DEV)
    return lax.dot_general(onehot, projected, (((0,), (0,)), ((), ())), preferred_element_type=jnp.float32)


def reference(misfit, block_counts, slot_element, observe, stokes_blocks, pattern, velocity, log_friction):
    by_owner = jnp.moveaxis(misfit, 1, 0)
    forcing = lax.map(lambda t: owner_forcing((t[0], t[1], t[2], observe)), (by_owner, block_counts, slot_element))
    forcing = forcing.reshape(N_GX, N_GY, EX, EY, BLK).transpose(0, 2, 1, 3, 4).reshape(NX, NY, BLK)
    forcing_b = forcing.astype(jnp.bfloat16)
    padded = jnp.pad(forcing_b, ((1, 1), (1, 1), (0, 0)))
    sources = []
    for k in range(9):
        p = k // 3 - 1
        q = k % 3 - 1
        sources.append(padded[1 - p:1 - p + NX, 1 - q:1 - q + NY])
    stacked = jnp.stack(sources, axis=2)
    stacked = jnp.where(pattern[:, :, :, None] == 1, stacked, jnp.zeros_like(stacked))
    adjoint = jnp.einsum("xyki,xykij->xyj", stacked.astype(jnp.float32), stokes_blocks.astype(jnp.float32), precision=lax.Precision.HIGHEST)
    fric = jnp.pad(log_friction, 1)
    beside = fric[2:, 1:-1] + fric[:-2, 1:-1] + fric[1:-1, 2:] + fric[1:-1, :-2]
    gradient = jnp.exp(log_friction) * jnp.sum(velocity.astype(jnp.float32) * adjoint, axis=2) + 0.5 * (4.0 * log_friction - beside)
    return adjoint, gradient
```

```python
import functools

import jax
import jax.numpy as jnp
from jax import lax
from jax.experimental import pallas as pl
from jax.experimental.pallas import tpu as pltpu
from jax.sharding import PartitionSpec as P

MESH = pl.DeviceIdType.MESH
F32 = jnp.float32
BF16 = jnp.bfloat16


def iota(shape, dim):
    return lax.broadcasted_iota(jnp.int32, shape, dim)


def kernel(
    nx, ny,
    misfit_hbm, counts_hbm, elem_hbm, obs_hbm, stokes_hbm, pat_hbm, vel_hbm, fric_hbm,
    adj_ref, grad_ref,
    misfit, counts, elem, obs, stokes, pat, vel, fric,
    outgoing, arrived, placed, onehot, present, cells, edge_l, edge_r, halo_t, halo_b, halo_l, halo_r,
    wide, near,
    in_sem, stokes_sem, send_sem, recv_sem, fric_send, fric_recv, halo_send, halo_recv,
):
    peers, slots, width = misfit.shape
    half = slots // 2
    rows_x, rows_y, offsets, blk, _ = stokes.shape
    elements = rows_x * rows_y
    lanes = 2 * blk
    gx, gy = lax.axis_index("gx"), lax.axis_index("gy")
    me = gx * ny + gy

    loads = [
        pltpu.make_async_copy(src, dst, in_sem.at[n])
        for n, (src, dst) in enumerate(
            (
                (misfit_hbm, misfit), (obs_hbm, obs), (fric_hbm, fric), (elem_hbm, elem),
                (counts_hbm, counts), (pat_hbm, pat), (vel_hbm, vel),
            )
        )
    ]
    for load in loads:
        load.start()

    for ref in (halo_t, halo_b, halo_l, halo_r, wide, near):
        ref[...] = jnp.zeros_like(ref)

    barrier = pltpu.get_barrier_semaphore()

    def greet(d, carry):
        peer = lax.rem(me + d, peers)
        pl.semaphore_signal(barrier, inc=1, device_id=(peer // ny, lax.rem(peer, ny)), device_id_type=MESH)
        return carry

    lax.fori_loop(1, peers, greet, 0)

    stokes_loads = [
        pltpu.make_async_copy(stokes_hbm.at[x], stokes.at[x], stokes_sem.at[x]) for x in range(rows_x)
    ]
    for load in stokes_loads:
        load.start()

    loads[0].wait()
    loads[1].wait()
    zeros = jnp.zeros_like(obs[...])
    weights = jnp.concatenate(
        [jnp.concatenate([obs[...], zeros], axis=1), jnp.concatenate([zeros, obs[...]], axis=1)], axis=0
    )

    def project(first, group):
        lo = misfit[pl.ds(first, group), :half, :].reshape(group * half, width)
        hi = misfit[pl.ds(first, group), half:, :].reshape(group * half, width)
        both = lax.dot_general(
            jnp.concatenate([lo, hi], axis=1), weights, (((1,), (1,)), ((), ())), preferred_element_type=F32
        )
        outgoing[pl.ds(first, group)] = both.astype(BF16).reshape(group, half, lanes)

    for s in range(nx):
        project(s * ny, ny)

    own = pltpu.make_async_copy(outgoing.at[me], arrived.at[me], recv_sem)
    own.start()
    pl.semaphore_wait(barrier, peers - 1)

    def send(d, carry):
        peer = lax.rem(me + d, peers)
        pltpu.make_async_remote_copy(
            src_ref=outgoing.at[peer], dst_ref=arrived.at[me], send_sem=send_sem, recv_sem=recv_sem,
            device_id=(peer // ny, lax.rem(peer, ny)), device_id_type=MESH,
        ).start()
        return carry

    lax.fori_loop(1, peers, send, 0)

    has = {"t": gx > 0, "b": gx < nx - 1, "l": gy > 0, "r": gy < ny - 1}

    cells[...] = jnp.zeros_like(cells)

    loads[2].wait()
    wide[:, :rows_y] = fric[...]
    faces = [("t", 1, -1, 0), ("b", 0, 1, 0), ("l", 3, 0, -1), ("r", 2, 0, 1)]
    slot_of = {"t": 0, "b": 1, "l": 2, "r": 3}
    fric_copies = []
    for side, slot, dx, dy in faces:
        fric_copies.append(
            (
                side,
                pltpu.make_async_remote_copy(
                    src_ref=wide, dst_ref=near.at[slot], send_sem=fric_send.at[slot], recv_sem=fric_recv.at[slot],
                    device_id=(gx + dx, gy + dy), device_id_type=MESH,
                ),
            )
        )
    for side, copy in fric_copies:
        pl.when(has[side])(copy.start)

    loads[3].wait()
    loads[4].wait()
    count = jnp.sum(
        jnp.where(iota((peers, peers), 0) == iota((peers, peers), 1), jnp.broadcast_to(counts[...], (peers, peers)), 0),
        axis=1, keepdims=True,
    )
    placed[:, :slots] = jnp.where(iota((peers, slots), 1) < count, elem[...], -1).astype(F32)
    per = lanes // half
    groups = peers // per
    rows = [jnp.zeros((groups, lanes), F32), jnp.zeros((groups, lanes), F32)]
    for j in range(per):
        part = placed[pl.ds(j, groups, stride=per), :][:, :slots].astype(BF16)
        for side in range(2):
            to = iota((slots, lanes), 0) - side * half
            place = (to >= 0) & (to < half) & (iota((slots, lanes), 1) == to + j * half)
            rows[side] = rows[side] + jnp.dot(
                part, jnp.where(place, 1.0, 0.0).astype(BF16), preferred_element_type=F32
            )
    which = iota((elements, lanes), 0).astype(F32)
    for side in range(2):
        for g in range(groups):
            row = jnp.broadcast_to(rows[side][g : g + 1, :], (elements, lanes))
            onehot[side * elements : (side + 1) * elements, g * lanes : (g + 1) * lanes] = jnp.where(
                which == row, 1.0, 0.0
            ).astype(BF16)

    loads[5].wait()
    eye = jnp.where(iota((rows_y, rows_y), 0) == iota((rows_y, rows_y), 1), 1.0, 0.0)
    ones = jnp.ones((rows_y, lanes), BF16)

    def spread(k, carry):
        now = pat[k].astype(F32)
        for x in range(rows_x):
            diagonal = (jnp.broadcast_to(now[x : x + 1, :], (rows_y, rows_y)) * eye).astype(BF16)
            present[k, x] = jnp.dot(diagonal, ones, preferred_element_type=F32).astype(BF16)
        return carry

    lax.fori_loop(0, offsets, spread, 0)

    pltpu.make_async_copy(arrived, arrived, recv_sem).wait()
    sums = jnp.zeros((2 * elements, lanes), F32)
    step = min(16, peers)
    for s in range(0, peers, step):
        sums = sums + jnp.dot(
            onehot[:, s * half : (s + step) * half],
            arrived[s : s + step].reshape(step * half, lanes),
            preferred_element_type=F32,
        )
    mixed = jnp.where(iota((elements, lanes), 1) < blk, sums[:elements], sums[elements:])
    forcing = (mixed + pltpu.roll(mixed, blk, axis=1)).astype(BF16).astype(F32)
    forcing = forcing.reshape(rows_x, rows_y, lanes)
    cells[1 : rows_x + 1, 8 : 8 + rows_y] = forcing
    for x in range(rows_x):
        edge_l[x : x + 1, :] = forcing[x, :1, :]
        edge_r[x : x + 1, :] = forcing[x, rows_y - 1 :, :]

    halo_copies = []

    def halo(n, cond, src, dst, dx, dy):
        out = pltpu.make_async_remote_copy(
            src_ref=src, dst_ref=dst, send_sem=halo_send.at[n], recv_sem=halo_recv.at[n],
            device_id=(gx + dx, gy + dy), device_id_type=MESH,
        )
        pl.when(cond)(out.start)
        halo_copies.append((n, cond, out))

    for n, dx, cond in ((2, -1, has["t"]), (6, 1, has["b"]), (4, 0, None)):
        for dy, side, edge, dst in ((-1, "l", edge_l, halo_r), (1, "r", edge_r, halo_l)):
            both = has[side] if cond is None else jnp.logical_and(cond, has[side])
            halo(n, both, edge, dst.at[pl.ds(rows_x * (1 - dx), rows_x)], dx, dy)
            n += 1
    halo(0, has["t"], cells.at[1, pl.ds(8, rows_y)], halo_b.at[pl.ds(8, rows_y)], -1, 0)
    halo(1, has["b"], cells.at[rows_x, pl.ds(8, rows_y)], halo_t.at[pl.ds(8, rows_y)], 1, 0)

    lane_block = iota((rows_y, lanes), 1) // blk
    row_of = iota((rows_y, lanes), 0)
    masks = [
        jnp.where(row_of == 2 * c + lane_block, 1.0, 0.0).astype(BF16) for c in range(rows_y // 2)
    ]

    def product(source, x, k):
        source = source.astype(BF16) * present[k, x]
        left = jnp.concatenate([source * mask for mask in masks], axis=1)
        right = stokes[x, :, k].reshape(rows_y * blk, blk)
        return jnp.dot(left, right, preferred_element_type=F32)

    for load in stokes_loads:
        load.wait()

    def row(x, carry):
        total = jnp.zeros((rows_y, blk), F32)
        for k in range(9):
            p, q = k // 3 - 1, k % 3 - 1
            total = total + product(cells[1 + x - p, 8 - q : 8 - q + rows_y, :], x, k)
        adj_ref[x] = total
        return carry

    lax.fori_loop(0, rows_x, row, 0)

    by_slot = {n: copy for n, cond, copy in halo_copies}
    arrivals = (
        (0, has["b"]), (1, has["t"]),
        (2, jnp.logical_and(has["b"], has["r"])), (3, jnp.logical_and(has["b"], has["l"])),
        (4, has["r"]), (5, has["l"]),
        (6, jnp.logical_and(has["t"], has["r"])), (7, jnp.logical_and(has["t"], has["l"])),
    )
    for n, cond in arrivals:
        pl.when(cond)(by_slot[n].wait_recv)
    for x, p, ref in ((0, 1, halo_t), (rows_x - 1, -1, halo_b)):
        total = adj_ref[x]
        for q in (-1, 0, 1):
            total = total + product(ref[8 - q : 8 - q + rows_y, :], x, (p + 1) * 3 + q + 1)
        adj_ref[x] = total

    pick = [
        jnp.where(iota((rows_x, lanes), 0) == 2 * c + iota((rows_x, lanes), 1) // blk, 1.0, 0.0)
        for c in range(rows_x // 2)
    ]
    for y, q, ref in ((0, 1, halo_l), (rows_y - 1, -1, halo_r)):
        total = jnp.zeros((rows_x, blk), F32)
        for p in (-1, 0, 1):
            k = (p + 1) * 3 + q + 1
            tags = jnp.concatenate(
                [present[k, x].astype(F32)[y : y + 1, :] for x in range(rows_x)], axis=0
            )
            source = ref[rows_x - p : 2 * rows_x - p, :] * tags
            left = jnp.concatenate([source * mask for mask in pick], axis=1).astype(BF16)
            right = stokes[:, y, k].reshape(rows_x * blk, blk)
            total = total + jnp.dot(left, right, preferred_element_type=F32)
        for x in range(rows_x):
            adj_ref[x, y : y + 1, :] = adj_ref[x, y : y + 1, :] + total[x : x + 1, :]

    loads[6].wait()
    for side, copy in fric_copies:
        pl.when(has[side])(copy.wait_send)
    for side, slot, dx, dy in faces:
        back = [c for c in fric_copies if c[0] == {"t": "b", "b": "t", "l": "r", "r": "l"}[side]][0][1]
        pl.when(has[side])(back.wait_recv)
    level = wide[...]
    row_id, lane_id = iota(level.shape, 0), iota(level.shape, 1)
    above = jnp.where(row_id == 0, pltpu.roll(near[0], 1, axis=0), pltpu.roll(level, 1, axis=0))
    below = jnp.where(
        row_id == rows_x - 1, pltpu.roll(near[1], rows_x - 1, axis=0), pltpu.roll(level, rows_x - 1, axis=0)
    )
    span = level.shape[1]
    before = jnp.where(
        lane_id == 0, pltpu.roll(near[2], span - rows_y + 1, axis=1), pltpu.roll(level, 1, axis=1)
    )
    after = jnp.where(
        lane_id == rows_y - 1, pltpu.roll(near[3], rows_y - 1, axis=1), pltpu.roll(level, span - 1, axis=1)
    )
    smooth = 0.5 * (4.0 * level - (above + below + before + after))
    work = []
    for x in range(rows_x):
        column = jnp.sum(vel[x].astype(F32) * adj_ref[x], axis=1, keepdims=True)
        work.append(jnp.sum(jnp.broadcast_to(column, (rows_y, rows_y)) * eye, axis=0, keepdims=True))
    work = jnp.concatenate(work, axis=0)
    grad_ref[...] = jnp.exp(fric[...]) * work + smooth[:, :rows_y]

    for n, cond, copy in halo_copies:
        pl.when(cond)(copy.wait_send)
    pltpu.make_async_copy(
        outgoing.at[pl.ds(0, peers - 1)], outgoing.at[pl.ds(0, peers - 1)], send_sem
    ).wait()


def hand_on(adj_in, grad_in, adj_out, grad_out, sem):
    copies = [
        pltpu.make_async_copy(adj_in, adj_out, sem.at[0]), pltpu.make_async_copy(grad_in, grad_out, sem.at[1])
    ]
    for copy in copies:
        copy.start()
    for copy in copies:
        copy.wait()


def per_device(
    nx, ny, misfit, block_counts, slot_element, observe, stokes_blocks, pattern, velocity, log_friction
):
    _, peers, slots, width = misfit.shape
    rows_x, rows_y, offsets, blk, _ = stokes_blocks.shape
    elements = rows_x * rows_y
    lanes = 2 * blk
    half = slots // 2
    args = (
        misfit[0], block_counts, slot_element[0], observe.T, stokes_blocks,
        pattern.transpose(2, 0, 1), velocity, log_friction,
    )
    vm = pltpu.VMEM
    made = pl.pallas_call(
        functools.partial(kernel, nx, ny),
        out_shape=(pltpu.VMEM((rows_x, rows_y, blk), F32), pltpu.VMEM((rows_x, rows_y), F32)),
        in_specs=[pl.BlockSpec(memory_space=pltpu.HBM)] * len(args),
        out_specs=(pl.BlockSpec(memory_space=pltpu.VMEM),) * 2,
        scratch_shapes=[vm(a.shape, a.dtype) for a in args]
        + [
            vm((peers, half, lanes), BF16),
            vm((peers, half, lanes), BF16),
            vm((peers, 128), F32),
            vm((2 * elements, peers * half), BF16),
            vm((offsets, rows_x, rows_y, lanes), BF16),
            vm((rows_x + 2, rows_y + 16, lanes), F32),
            vm((rows_x, lanes), F32),
            vm((rows_x, lanes), F32),
            vm((rows_y + 16, lanes), F32),
            vm((rows_y + 16, lanes), F32),
            vm((3 * rows_x, lanes), F32),
            vm((3 * rows_x, lanes), F32),
            vm((rows_x, 128), F32),
            vm((4, rows_x, 128), F32),
            pltpu.SemaphoreType.DMA((7,)),
            pltpu.SemaphoreType.DMA((rows_x,)),
            pltpu.SemaphoreType.DMA,
            pltpu.SemaphoreType.DMA,
            pltpu.SemaphoreType.DMA((4,)),
            pltpu.SemaphoreType.DMA((4,)),
            pltpu.SemaphoreType.DMA((8,)),
            pltpu.SemaphoreType.DMA((8,)),
        ],
        compiler_params=pltpu.CompilerParams(
            collective_id=0, has_side_effects=True, vmem_limit_bytes=60 * 1024 * 1024
        ),
    )(*args)
    return pl.pallas_call(
        hand_on,
        out_shape=tuple(jax.ShapeDtypeStruct(a.shape, a.dtype) for a in made),
        in_specs=[pl.BlockSpec(memory_space=pltpu.VMEM)] * 2,
        out_specs=(pl.BlockSpec(memory_space=pltpu.HBM),) * 2,
        scratch_shapes=[pltpu.SemaphoreType.DMA((2,))],
        compiler_params=pltpu.CompilerParams(vmem_limit_bytes=1024 * 1024),
    )(*made)


def solution(mesh):
    in_specs = (
        P(("gx", "gy"), None, None, None),
        P(("gx", "gy"), None),
        P(("gx", "gy"), None, None),
        P(),
        P("gx", "gy", None, None, None),
        P("gx", "gy", None),
        P("gx", "gy", None),
        P("gx", "gy"),
    )
    out_specs = (P("gx", "gy", None), P("gx", "gy"))
    return jax.shard_map(
        functools.partial(per_device, mesh.shape["gx"], mesh.shape["gy"]),
        mesh=mesh, in_specs=in_specs, out_specs=out_specs, check_vma=False,
    )
```

```python
import functools

import jax
import jax.numpy as jnp
from jax import lax
from jax.experimental import pallas as pl
from jax.experimental.pallas import tpu as pltpu
from jax.sharding import PartitionSpec as P

MESH = pl.DeviceIdType.MESH
F32 = jnp.float32
BF16 = jnp.bfloat16


def iota(shape, dim):
    return lax.broadcasted_iota(jnp.int32, shape, dim)


def kernel(
    nx, ny,
    misfit_hbm, counts_hbm, elem_hbm, obs_hbm, stokes_hbm, pat_hbm, vel_hbm, fric_hbm,
    adj_ref, grad_ref,
    misfit, counts, elem, obs, stokes, pat, vel, fric,
    outgoing, arrived, placed, table_out, table_in, onehot, present, partial, window_out, window_in,
    edge_out, edge_in, cells, shifted, wide, near,
    misfit_sem, in_sem, stokes_sem, send_sem, recv_sem, table_send, table_recv, fric_send, fric_recv,
    window_send, window_recv, edge_send, edge_recv, vouch, packed,
):
    peers, slots, width = misfit.shape
    half = slots // 2
    rows_x, rows_y, offsets, blk, _ = stokes.shape
    elements = rows_x * rows_y
    lanes = 2 * blk
    reach = rows_x + 2
    gx, gy = lax.axis_index("gx"), lax.axis_index("gy")
    has = {"t": gx > 0, "b": gx < nx - 1, "l": gy > 0, "r": gy < ny - 1}

    high = (2 * gx) // nx
    order = [(1 - high) * (nx - 1 - c) + high * c for c in range(nx)]

    misfit_loads = [
        pltpu.make_async_copy(
            misfit_hbm.at[pl.ds(order[c] * ny, ny)], misfit.at[pl.ds(order[c] * ny, ny)], misfit_sem.at[c]
        )
        for c in range(nx)
    ]
    loads = [
        pltpu.make_async_copy(src, dst, in_sem.at[n])
        for n, (src, dst) in enumerate(
            ((obs_hbm, obs), (elem_hbm, elem), (counts_hbm, counts), (fric_hbm, fric), (pat_hbm, pat), (vel_hbm, vel))
        )
    ]
    for load in loads[:3] + misfit_loads + loads[3:]:
        load.start()

    for ref in (wide, near):
        ref[...] = jnp.zeros_like(ref)

    barrier = pltpu.get_barrier_semaphore()

    def greet(x, y):
        pl.semaphore_signal(barrier, inc=1, device_id=(x, y), device_id_type=MESH)

    for d in range(1, nx):
        greet(lax.rem(gx + d, nx), gy)
    for d in range(1, ny):
        greet(gx, lax.rem(gy + d, ny))

    stokes_loads = [
        pltpu.make_async_copy(stokes_hbm.at[x], stokes.at[x], stokes_sem.at[x]) for x in range(rows_x)
    ]
    for load in stokes_loads:
        load.start()

    partial[pl.ds(0, rows_y), :] = jnp.zeros((rows_y, lanes), F32)
    below = partial.shape[0] - (nx * rows_x + 1) * rows_y
    partial[pl.ds((nx * rows_x + 1) * rows_y, below), :] = jnp.zeros((below, lanes), F32)

    def no_edge(side):
        edge_in[side] = jnp.zeros_like(edge_in[side])

    pl.when(gy == 0)(functools.partial(no_edge, 0))
    pl.when(gy == ny - 1)(functools.partial(no_edge, 1))

    loads[1].wait()
    loads[2].wait()
    count = jnp.sum(
        jnp.where(iota((peers, peers), 0) == iota((peers, peers), 1), jnp.broadcast_to(counts[...], (peers, peers)), 0),
        axis=1, keepdims=True,
    )
    placed[:, :slots] = jnp.where(iota((peers, slots), 1) < count, elem[...], -1).astype(F32)
    per = lanes // half
    groups = peers // per
    own_groups = groups // nx
    rows = [jnp.zeros((groups, lanes), F32), jnp.zeros((groups, lanes), F32)]
    for j in range(per):
        part = placed[pl.ds(j, groups, stride=per), :][:, :slots].astype(BF16)
        for side in range(2):
            to = iota((slots, lanes), 0) - side * half
            place = (to >= 0) & (to < half) & (iota((slots, lanes), 1) == to + j * half)
            rows[side] = rows[side] + jnp.dot(
                part, jnp.where(place, 1.0, 0.0).astype(BF16), preferred_element_type=F32
            )
    table_out[...] = jnp.zeros_like(table_out)
    for i in range(nx):
        for side in range(2):
            table_out[i, side * own_groups : (side + 1) * own_groups, :] = rows[side][
                i * own_groups : (i + 1) * own_groups, :
            ]
    table_in[gx] = table_out[gx]

    loads[0].wait()
    zeros = jnp.zeros_like(obs[...])
    weights = jnp.concatenate(
        [jnp.concatenate([obs[...], zeros], axis=1), jnp.concatenate([zeros, obs[...]], axis=1)], axis=0
    )

    def project(c):
        misfit_loads[c].wait()
        first = order[c] * ny
        lo = misfit[pl.ds(first, ny), :half, :].reshape(ny * half, width)
        hi = misfit[pl.ds(first, ny), half:, :].reshape(ny * half, width)
        both = lax.dot_general(
            jnp.concatenate([lo, hi], axis=1), weights, (((1,), (1,)), ((), ())), preferred_element_type=F32
        )
        outgoing[order[c]] = both.astype(BF16).reshape(ny, half, lanes)

    project(0)

    loads[3].wait()
    wide[:, :rows_y] = fric[...]
    faces = [("t", 1, -1, 0), ("b", 0, 1, 0), ("l", 3, 0, -1), ("r", 2, 0, 1)]
    fric_copies = []
    for side, slot, dx, dy in faces:
        fric_copies.append(
            (
                side,
                pltpu.make_async_remote_copy(
                    src_ref=wide, dst_ref=near.at[slot], send_sem=fric_send.at[slot], recv_sem=fric_recv.at[slot],
                    device_id=(gx + dx, gy + dy), device_id_type=MESH,
                ),
            )
        )
    pl.semaphore_wait(barrier, nx + ny - 2)
    for d in range(1, nx):
        pl.semaphore_signal(vouch, inc=1, device_id=(lax.rem(gx + d, nx), gy), device_id_type=MESH)
    for d in range(1, nx):
        other = lax.rem(gx + d, nx)
        pltpu.make_async_remote_copy(
            src_ref=table_out.at[other], dst_ref=table_in.at[gx], send_sem=table_send, recv_sem=table_recv,
            device_id=(other, gy), device_id_type=MESH,
        ).start()

    for c in range(nx):
        if c > 0:
            project(c)

        def send(d, carry, c=c):
            peer = lax.rem(gy + d, ny)
            pltpu.make_async_remote_copy(
                src_ref=outgoing.at[order[c], peer], dst_ref=arrived.at[order[c], gy],
                send_sem=send_sem, recv_sem=recv_sem.at[c], device_id=(gx, peer), device_id_type=MESH,
            ).start()
            return carry

        lax.fori_loop(1, ny, send, 0)

    for side, copy in fric_copies:
        pl.when(has[side])(copy.start)

    for c in range(nx):
        arrived[order[c], gy] = outgoing[order[c], gy]

    def pack(first, last):
        for x in range(first, last):
            stokes_loads[x].wait()
            packed[x] = jnp.concatenate([stokes[x, : rows_y // 2], stokes[x, rows_y // 2 :]], axis=-1)

    pack(0, 2)

    table_all = table_in.at[pl.ds(0, nx - 1)]
    pltpu.make_async_copy(table_all, table_all, table_recv).wait()
    which = iota((elements, lanes), 0).astype(F32)
    for i in range(nx):
        for side in range(2):
            for g in range(own_groups):
                row = jnp.broadcast_to(table_in[i, side * own_groups + g : side * own_groups + g + 1, :], (elements, lanes))
                onehot[i, side * elements : (side + 1) * elements, g * lanes : (g + 1) * lanes] = jnp.where(
                    which == row, 1.0, 0.0
                ).astype(BF16)

    pl.semaphore_wait(vouch, nx - 1)
    left_lanes = iota((elements, lanes), 1) < blk
    span = reach * rows_y // 2
    window_lanes = iota((span, lanes), 1) < blk

    def pass_on(to):
        first = to * elements
        one = partial[pl.ds(first, span), :]
        two = partial[pl.ds(first + span, span), :]
        window = jnp.where(window_lanes, one, two).astype(BF16)

        def keep():
            window_in[gx] = window

        def give():
            window_out[to] = window
            pltpu.make_async_remote_copy(
                src_ref=window_out.at[to], dst_ref=window_in.at[gx], send_sem=window_send, recv_sem=window_recv,
                device_id=(to, gy), device_id_type=MESH,
            ).start()

        pl.when(to == gx)(keep)
        pl.when(to != gx)(give)
        for side, there, dy, column in ((0, "r", 1, rows_y - 1), (1, "l", -1, 0)):
            edge_out[side, to] = partial[pl.ds(first + column, 16, stride=rows_y), :].astype(BF16)

            def give_edge(side=side, dy=dy):
                pltpu.make_async_remote_copy(
                    src_ref=edge_out.at[side, to], dst_ref=edge_in.at[side, gx],
                    send_sem=edge_send.at[side], recv_sem=edge_recv.at[side],
                    device_id=(to, gy + dy), device_id_type=MESH,
                ).start()

            pl.when(has[there])(give_edge)

    for c in range(nx):
        now = order[c]
        landed = arrived.at[now, pl.ds(0, ny - 1)]
        pltpu.make_async_copy(landed, landed, recv_sem.at[c]).wait()
        sums = jnp.dot(
            onehot[now], arrived[now].reshape(ny * half, lanes), preferred_element_type=F32
        )
        mixed = jnp.where(left_lanes, sums[:elements], sums[elements:])
        partial[pl.ds(rows_y + now * elements, elements), :] = mixed + pltpu.roll(mixed, blk, axis=1)
        if c > 0:
            pass_on(order[c - 1])
    pass_on(order[nx - 1])

    loads[4].wait()
    eye = jnp.where(iota((rows_y, rows_y), 0) == iota((rows_y, rows_y), 1), 1.0, 0.0)
    tags = pat[...].astype(F32).reshape(offsets * rows_x, rows_y)
    tags = jnp.broadcast_to(tags[:, None, :], (offsets * rows_x, rows_y, rows_y)) * eye[None]
    spread = jnp.dot(
        tags.reshape(offsets * elements, rows_y).astype(BF16), jnp.ones((rows_y, lanes), BF16),
        preferred_element_type=F32,
    )
    present[...] = spread.astype(BF16).reshape(offsets, rows_x, rows_y, lanes)
    pack(2, rows_x)

    window_all = window_in.at[pl.ds(0, nx - 1)]
    pltpu.make_async_copy(window_all, window_all, window_recv).wait()
    total = window_in[0].astype(F32)
    for i in range(1, nx):
        total = total + window_in[i].astype(F32)
    turned = pltpu.roll(total, blk, axis=1)
    for part, rows_of in enumerate((jnp.where(window_lanes, total, turned), jnp.where(window_lanes, turned, total))):
        for r in range(reach // 2):
            cells[part * (reach // 2) + r, 8 : 8 + rows_y] = rows_of[r * rows_y : (r + 1) * rows_y]
    for side, there, at in ((0, "l", 7), (1, "r", 8 + rows_y)):
        edges = pltpu.make_async_copy(edge_in.at[side], edge_in.at[side], edge_recv.at[side])
        pl.when(has[there])(edges.wait)
        edge = edge_in[side, 0].astype(F32)
        for i in range(1, nx):
            edge = edge + edge_in[side, i].astype(F32)
        for r in range(reach):
            cells[r, at : at + 1, :] = edge[r : r + 1, :]
    for q in (-1, 0, 1):
        for r in range(reach):
            shifted[q + 1, r] = cells[r, 8 - q : 8 - q + rows_y, :].astype(BF16)

    lane_block = iota((rows_y, lanes), 1) // blk
    row_of = iota((rows_y, lanes), 0)
    masks = [
        jnp.where(lax.rem(row_of, rows_y // 2) == 2 * c + lane_block, 1.0, 0.0).astype(BF16)
        for c in range(rows_y // 4)
    ]

    def row(x, carry):
        total = jnp.zeros((rows_y, lanes), F32)
        for k in range(9):
            p, q = k // 3 - 1, k % 3 - 1
            source = shifted[q + 1, 1 + x - p] * present[k, x]
            left = jnp.concatenate([source * mask for mask in masks], axis=1)
            right = packed[x, :, k].reshape(rows_y // 2 * blk, lanes)
            total = total + jnp.dot(left, right, preferred_element_type=F32)
        adj_ref[x] = jnp.where(row_of < rows_y // 2, total, pltpu.roll(total, blk, axis=1))[:, :blk]
        return carry

    lax.fori_loop(0, rows_x, row, 0, unroll=8)

    loads[5].wait()
    for side, copy in fric_copies:
        pl.when(has[side])(copy.wait_send)
    for side, slot, dx, dy in faces:
        back = [c for c in fric_copies if c[0] == {"t": "b", "b": "t", "l": "r", "r": "l"}[side]][0][1]
        pl.when(has[side])(back.wait_recv)
    level = wide[...]
    row_id, lane_id = iota(level.shape, 0), iota(level.shape, 1)
    above = jnp.where(row_id == 0, pltpu.roll(near[0], 1, axis=0), pltpu.roll(level, 1, axis=0))
    below = jnp.where(
        row_id == rows_x - 1, pltpu.roll(near[1], rows_x - 1, axis=0), pltpu.roll(level, rows_x - 1, axis=0)
    )
    width_f = level.shape[1]
    before = jnp.where(
        lane_id == 0, pltpu.roll(near[2], width_f - rows_y + 1, axis=1), pltpu.roll(level, 1, axis=1)
    )
    after = jnp.where(
        lane_id == rows_y - 1, pltpu.roll(near[3], rows_y - 1, axis=1), pltpu.roll(level, width_f - 1, axis=1)
    )
    smooth = 0.5 * (4.0 * level - (above + below + before + after))
    work = []
    for x in range(rows_x):
        column = jnp.sum(vel[x].astype(F32) * adj_ref[x], axis=1, keepdims=True)
        work.append(jnp.sum(jnp.broadcast_to(column, (rows_y, rows_y)) * eye, axis=0, keepdims=True))
    work = jnp.concatenate(work, axis=0)
    grad_ref[...] = jnp.exp(fric[...]) * work + smooth[:, :rows_y]

    sent = outgoing.at[:, pl.ds(0, ny - 1)]
    pltpu.make_async_copy(sent, sent, send_sem).wait()
    table_all = table_out.at[pl.ds(0, nx - 1)]
    pltpu.make_async_copy(table_all, table_all, table_send).wait()
    window_all = window_out.at[pl.ds(0, nx - 1)]
    pltpu.make_async_copy(window_all, window_all, window_send).wait()
    for side, there in ((0, "r"), (1, "l")):
        edges = pltpu.make_async_copy(edge_out.at[side], edge_out.at[side], edge_send.at[side])
        pl.when(has[there])(edges.wait)


def hand_on(adj_in, grad_in, adj_out, grad_out, sem):
    copies = [
        pltpu.make_async_copy(adj_in, adj_out, sem.at[0]), pltpu.make_async_copy(grad_in, grad_out, sem.at[1])
    ]
    for copy in copies:
        copy.start()
    for copy in copies:
        copy.wait()


def per_device(
    nx, ny, misfit, block_counts, slot_element, observe, stokes_blocks, pattern, velocity, log_friction
):
    _, peers, slots, width = misfit.shape
    rows_x, rows_y, offsets, blk, _ = stokes_blocks.shape
    elements = rows_x * rows_y
    lanes = 2 * blk
    half = slots // 2
    args = (
        misfit[0], block_counts, slot_element[0], observe.T, stokes_blocks,
        pattern.transpose(2, 0, 1), velocity, log_friction,
    )
    table = -(-2 * ny * half // (8 * lanes)) * 8
    vm, dma = pltpu.VMEM, pltpu.SemaphoreType.DMA
    made = pl.pallas_call(
        functools.partial(kernel, nx, ny),
        out_shape=(pltpu.VMEM((rows_x, rows_y, blk), F32), pltpu.VMEM((rows_x, rows_y), F32)),
        in_specs=[pl.BlockSpec(memory_space=pltpu.HBM)] * len(args),
        out_specs=(pl.BlockSpec(memory_space=pltpu.VMEM),) * 2,
        scratch_shapes=[vm(a.shape, a.dtype) for a in args]
        + [
            vm((nx, ny, half, lanes), BF16),
            vm((nx, ny, half, lanes), BF16),
            vm((peers, 128), F32),
            vm((nx, table, lanes), F32),
            vm((nx, table, lanes), F32),
            vm((nx, 2 * elements, ny * half), BF16),
            vm((offsets, rows_x, rows_y, lanes), BF16),
            vm(((nx * rows_x + 8 + 2) * rows_y, lanes), F32),
            vm((nx, (rows_x + 2) * rows_y // 2, lanes), BF16),
            vm((nx, (rows_x + 2) * rows_y // 2, lanes), BF16),
            vm((2, nx, 16, lanes), BF16),
            vm((2, nx, 16, lanes), BF16),
            vm((rows_x + 2, rows_y + 16, lanes), F32),
            vm((3, rows_x + 2, rows_y, lanes), BF16),
            vm((rows_x, 128), F32),
            vm((4, rows_x, 128), F32),
            dma((nx,)),
            dma((6,)),
            dma((rows_x,)),
            dma,
            dma((nx,)),
            dma,
            dma,
            dma((4,)),
            dma((4,)),
            dma,
            dma,
            dma((2,)),
            dma((2,)),
            pltpu.SemaphoreType.REGULAR,
            vm((rows_x, rows_y // 2, offsets, blk, lanes), BF16),
        ],
        compiler_params=pltpu.CompilerParams(
            collective_id=0, has_side_effects=True, vmem_limit_bytes=60 * 1024 * 1024
        ),
    )(*args)
    return pl.pallas_call(
        hand_on,
        out_shape=tuple(jax.ShapeDtypeStruct(a.shape, a.dtype) for a in made),
        in_specs=[pl.BlockSpec(memory_space=pltpu.VMEM)] * 2,
        out_specs=(pl.BlockSpec(memory_space=pltpu.HBM),) * 2,
        scratch_shapes=[pltpu.SemaphoreType.DMA((2,))],
        compiler_params=pltpu.CompilerParams(vmem_limit_bytes=1024 * 1024),
    )(*made)


def solution(mesh):
    in_specs = (
        P(("gx", "gy"), None, None, None),
        P(("gx", "gy"), None),
        P(("gx", "gy"), None, None),
        P(),
        P("gx", "gy", None, None, None),
        P("gx", "gy", None),
        P("gx", "gy", None),
        P("gx", "gy"),
    )
    out_specs = (P("gx", "gy", None), P("gx", "gy"))
    return jax.shard_map(
        functools.partial(per_device, mesh.shape["gx"], mesh.shape["gy"]),
        mesh=mesh, in_specs=in_specs, out_specs=out_specs, check_vma=False,
    )
```

```python
import functools

import jax
import jax.numpy as jnp
from jax import lax
from jax.experimental import pallas as pl
from jax.experimental.pallas import tpu as pltpu
from jax.sharding import PartitionSpec as P

MESH = pl.DeviceIdType.MESH
F32 = jnp.float32
BF16 = jnp.bfloat16


def iota(shape, dim):
    return lax.broadcasted_iota(jnp.int32, shape, dim)


def kernel(
    nx, ny,
    misfit_hbm, counts_hbm, elem_hbm, obs_hbm, stokes_hbm, pat_hbm, vel_hbm, fric_hbm,
    adj_ref, grad_ref,
    misfit, counts, elem, obs, stokes, pat, vel, fric,
    outgoing, arrived, placed, table_out, table_in, onehot, present, partial, window_out, window_in,
    edge_out, edge_in, cells, shifted, wide, near,
    misfit_sem, in_sem, stokes_sem, send_sem, recv_sem, table_send, table_recv, fric_send, fric_recv,
    window_send, window_recv, edge_send, edge_recv, vouch, packed,
):
    peers, slots, width = misfit.shape
    half = slots // 2
    rows_x, rows_y, offsets, blk, _ = stokes.shape
    elements = rows_x * rows_y
    lanes = 2 * blk
    reach = rows_x + 2
    gx, gy = lax.axis_index("gx"), lax.axis_index("gy")
    has = {"t": gx > 0, "b": gx < nx - 1, "l": gy > 0, "r": gy < ny - 1}

    high = (gx + nx - 1) // nx
    order = [(1 - high) * (nx - 1 - c) + high * c for c in range(nx)]

    misfit_loads = [
        pltpu.make_async_copy(
            misfit_hbm.at[pl.ds(order[c] * ny, ny)], misfit.at[pl.ds(order[c] * ny, ny)], misfit_sem.at[c]
        )
        for c in range(nx)
    ]
    loads = [
        pltpu.make_async_copy(src, dst, in_sem.at[n])
        for n, (src, dst) in enumerate(
            ((obs_hbm, obs), (elem_hbm, elem), (counts_hbm, counts), (fric_hbm, fric), (pat_hbm, pat), (vel_hbm, vel))
        )
    ]
    for load in loads[:3] + misfit_loads + loads[3:]:
        load.start()

    for ref in (wide, near):
        ref[...] = jnp.zeros_like(ref)

    barrier = pltpu.get_barrier_semaphore()

    def greet(x, y):
        pl.semaphore_signal(barrier, inc=1, device_id=(x, y), device_id_type=MESH)

    for d in range(1, nx):
        greet(lax.rem(gx + d, nx), gy)
    for d in range(1, ny):
        greet(gx, lax.rem(gy + d, ny))

    stokes_loads = [
        pltpu.make_async_copy(stokes_hbm.at[x], stokes.at[x], stokes_sem.at[x]) for x in range(rows_x)
    ]
    for load in stokes_loads:
        load.start()

    partial[pl.ds(0, rows_y), :] = jnp.zeros((rows_y, lanes), F32)
    below = partial.shape[0] - (nx * rows_x + 1) * rows_y
    partial[pl.ds((nx * rows_x + 1) * rows_y, below), :] = jnp.zeros((below, lanes), F32)

    def no_edge(side):
        edge_in[side] = jnp.zeros_like(edge_in[side])

    pl.when(gy == 0)(functools.partial(no_edge, 0))
    pl.when(gy == ny - 1)(functools.partial(no_edge, 1))

    loads[1].wait()
    loads[2].wait()
    count = jnp.sum(
        jnp.where(iota((peers, peers), 0) == iota((peers, peers), 1), jnp.broadcast_to(counts[...], (peers, peers)), 0),
        axis=1, keepdims=True,
    )
    placed[:, :slots] = jnp.where(iota((peers, slots), 1) < count, elem[...], -1).astype(F32)
    per = lanes // half
    groups = peers // per
    own_groups = groups // nx
    rows = [jnp.zeros((groups, lanes), F32), jnp.zeros((groups, lanes), F32)]
    for j in range(per):
        part = placed[pl.ds(j, groups, stride=per), :][:, :slots].astype(BF16)
        for side in range(2):
            to = iota((slots, lanes), 0) - side * half
            place = (to >= 0) & (to < half) & (iota((slots, lanes), 1) == to + j * half)
            rows[side] = rows[side] + jnp.dot(
                part, jnp.where(place, 1.0, 0.0).astype(BF16), preferred_element_type=F32
            )
    table_out[...] = jnp.zeros_like(table_out)
    for i in range(nx):
        for side in range(2):
            table_out[i, side * own_groups : (side + 1) * own_groups, :] = rows[side][
                i * own_groups : (i + 1) * own_groups, :
            ]
    table_in[gx] = table_out[gx]

    loads[0].wait()
    zeros = jnp.zeros_like(obs[...])
    weights = jnp.concatenate(
        [jnp.concatenate([obs[...], zeros], axis=1), jnp.concatenate([zeros, obs[...]], axis=1)], axis=0
    )

    def project(c):
        misfit_loads[c].wait()
        first = order[c] * ny
        lo = misfit[pl.ds(first, ny), :half, :].reshape(ny * half, width)
        hi = misfit[pl.ds(first, ny), half:, :].reshape(ny * half, width)
        both = lax.dot_general(
            jnp.concatenate([lo, hi], axis=1), weights, (((1,), (1,)), ((), ())), preferred_element_type=F32
        )
        outgoing[order[c]] = both.astype(BF16).reshape(ny, half, lanes)

    project(0)

    loads[3].wait()
    wide[:, :rows_y] = fric[...]
    faces = [("t", 1, -1, 0), ("b", 0, 1, 0), ("l", 3, 0, -1), ("r", 2, 0, 1)]
    fric_copies = []
    for side, slot, dx, dy in faces:
        fric_copies.append(
            (
                side,
                pltpu.make_async_remote_copy(
                    src_ref=wide, dst_ref=near.at[slot], send_sem=fric_send.at[slot], recv_sem=fric_recv.at[slot],
                    device_id=(gx + dx, gy + dy), device_id_type=MESH,
                ),
            )
        )
    pl.semaphore_wait(barrier, nx + ny - 2)
    for d in range(1, nx):
        pl.semaphore_signal(vouch, inc=1, device_id=(lax.rem(gx + d, nx), gy), device_id_type=MESH)
    for d in range(1, nx):
        other = lax.rem(gx + d, nx)
        pltpu.make_async_remote_copy(
            src_ref=table_out.at[other], dst_ref=table_in.at[gx], send_sem=table_send, recv_sem=table_recv,
            device_id=(other, gy), device_id_type=MESH,
        ).start()

    for c in range(nx):
        if c > 0:
            project(c)

        def send(d, carry, c=c):
            peer = lax.rem(gy + d, ny)
            pltpu.make_async_remote_copy(
                src_ref=outgoing.at[order[c], peer], dst_ref=arrived.at[order[c], gy],
                send_sem=send_sem, recv_sem=recv_sem.at[c], device_id=(gx, peer), device_id_type=MESH,
            ).start()
            return carry

        lax.fori_loop(1, ny, send, 0)

    for side, copy in fric_copies:
        pl.when(has[side])(copy.start)

    for c in range(nx):
        arrived[order[c], gy] = outgoing[order[c], gy]

    def pack(first, last):
        for x in range(first, last):
            stokes_loads[x].wait()
            packed[x] = jnp.concatenate([stokes[x, : rows_y // 2], stokes[x, rows_y // 2 :]], axis=-1)

    pack(0, 5)

    table_all = table_in.at[pl.ds(0, nx - 1)]
    pltpu.make_async_copy(table_all, table_all, table_recv).wait()
    which = iota((elements, lanes), 0).astype(F32)
    for i in range(nx):
        for side in range(2):
            for g in range(own_groups):
                row = jnp.broadcast_to(table_in[i, side * own_groups + g : side * own_groups + g + 1, :], (elements, lanes))
                onehot[i, side * elements : (side + 1) * elements, g * lanes : (g + 1) * lanes] = jnp.where(
                    which == row, 1.0, 0.0
                ).astype(BF16)

    pl.semaphore_wait(vouch, nx - 1)
    left_lanes = iota((elements, lanes), 1) < blk
    span = reach * rows_y // 2
    window_lanes = iota((span, lanes), 1) < blk

    def pass_on(to):
        first = to * elements
        one = partial[pl.ds(first, span), :]
        two = partial[pl.ds(first + span, span), :]
        window = jnp.where(window_lanes, one, two).astype(BF16)

        def keep():
            window_in[gx] = window

        def give():
            window_out[to] = window
            pltpu.make_async_remote_copy(
                src_ref=window_out.at[to], dst_ref=window_in.at[gx], send_sem=window_send, recv_sem=window_recv,
                device_id=(to, gy), device_id_type=MESH,
            ).start()

        pl.when(to == gx)(keep)
        pl.when(to != gx)(give)
        for side, there, dy, column in ((0, "r", 1, rows_y - 1), (1, "l", -1, 0)):
            edge_out[side, to] = partial[pl.ds(first + column, 16, stride=rows_y), :].astype(BF16)

            def give_edge(side=side, dy=dy):
                pltpu.make_async_remote_copy(
                    src_ref=edge_out.at[side, to], dst_ref=edge_in.at[side, gx],
                    send_sem=edge_send.at[side], recv_sem=edge_recv.at[side],
                    device_id=(to, gy + dy), device_id_type=MESH,
                ).start()

            pl.when(has[there])(give_edge)

    for c in range(nx):
        now = order[c]
        landed = arrived.at[now, pl.ds(0, ny - 1)]
        pltpu.make_async_copy(landed, landed, recv_sem.at[c]).wait()
        sums = jnp.dot(
            onehot[now], arrived[now].reshape(ny * half, lanes), preferred_element_type=F32
        )
        mixed = jnp.where(left_lanes, sums[:elements], sums[elements:])
        partial[pl.ds(rows_y + now * elements, elements), :] = mixed + pltpu.roll(mixed, blk, axis=1)
        if c > 0:
            pass_on(order[c - 1])
    pass_on(order[nx - 1])

    loads[4].wait()
    eye = jnp.where(iota((rows_y, rows_y), 0) == iota((rows_y, rows_y), 1), 1.0, 0.0)
    tags = pat[...].astype(F32).reshape(offsets * rows_x, rows_y)
    tags = jnp.broadcast_to(tags[:, None, :], (offsets * rows_x, rows_y, rows_y)) * eye[None]
    spread = jnp.dot(
        tags.reshape(offsets * elements, rows_y).astype(BF16), jnp.ones((rows_y, lanes), BF16),
        preferred_element_type=F32,
    )
    present[...] = spread.astype(BF16).reshape(offsets, rows_x, rows_y, lanes)
    pack(5, rows_x)

    window_all = window_in.at[pl.ds(0, nx - 1)]
    pltpu.make_async_copy(window_all, window_all, window_recv).wait()
    total = window_in[0].astype(F32)
    for i in range(1, nx):
        total = total + window_in[i].astype(F32)
    turned = pltpu.roll(total, blk, axis=1)
    for part, rows_of in enumerate((jnp.where(window_lanes, total, turned), jnp.where(window_lanes, turned, total))):
        for r in range(reach // 2):
            cells[part * (reach // 2) + r, 8 : 8 + rows_y] = rows_of[r * rows_y : (r + 1) * rows_y]
    for side, there, at in ((0, "l", 7), (1, "r", 8 + rows_y)):
        edges = pltpu.make_async_copy(edge_in.at[side], edge_in.at[side], edge_recv.at[side])
        pl.when(has[there])(edges.wait)
        edge = edge_in[side, 0].astype(F32)
        for i in range(1, nx):
            edge = edge + edge_in[side, i].astype(F32)
        for r in range(reach):
            cells[r, at : at + 1, :] = edge[r : r + 1, :]
    for q in (-1, 0, 1):
        for r in range(reach):
            shifted[q + 1, r] = cells[r, 8 - q : 8 - q + rows_y, :].astype(BF16)

    lane_block = iota((rows_y, lanes), 1) // blk
    row_of = iota((rows_y, lanes), 0)
    masks = [
        jnp.where(lax.rem(row_of, rows_y // 2) == 2 * c + lane_block, 1.0, 0.0).astype(BF16)
        for c in range(rows_y // 4)
    ]

    def row(x, carry):
        total = jnp.zeros((rows_y, lanes), F32)
        for k in range(9):
            p, q = k // 3 - 1, k % 3 - 1
            source = shifted[q + 1, 1 + x - p] * present[k, x]
            left = jnp.concatenate([source * mask for mask in masks], axis=1)
            right = packed[x, :, k].reshape(rows_y // 2 * blk, lanes)
            total = total + jnp.dot(left, right, preferred_element_type=F32)
        adj_ref[x] = jnp.where(row_of < rows_y // 2, total, pltpu.roll(total, blk, axis=1))[:, :blk]
        return carry

    lax.fori_loop(0, rows_x, row, 0, unroll=8)

    loads[5].wait()
    for side, copy in fric_copies:
        pl.when(has[side])(copy.wait_send)
    for side, slot, dx, dy in faces:
        back = [c for c in fric_copies if c[0] == {"t": "b", "b": "t", "l": "r", "r": "l"}[side]][0][1]
        pl.when(has[side])(back.wait_recv)
    level = wide[...]
    row_id, lane_id = iota(level.shape, 0), iota(level.shape, 1)
    above = jnp.where(row_id == 0, pltpu.roll(near[0], 1, axis=0), pltpu.roll(level, 1, axis=0))
    below = jnp.where(
        row_id == rows_x - 1, pltpu.roll(near[1], rows_x - 1, axis=0), pltpu.roll(level, rows_x - 1, axis=0)
    )
    width_f = level.shape[1]
    before = jnp.where(
        lane_id == 0, pltpu.roll(near[2], width_f - rows_y + 1, axis=1), pltpu.roll(level, 1, axis=1)
    )
    after = jnp.where(
        lane_id == rows_y - 1, pltpu.roll(near[3], rows_y - 1, axis=1), pltpu.roll(level, width_f - 1, axis=1)
    )
    smooth = 0.5 * (4.0 * level - (above + below + before + after))
    work = []
    for x in range(rows_x):
        column = jnp.sum(vel[x].astype(F32) * adj_ref[x], axis=1, keepdims=True)
        work.append(jnp.sum(jnp.broadcast_to(column, (rows_y, rows_y)) * eye, axis=0, keepdims=True))
    work = jnp.concatenate(work, axis=0)
    grad_ref[...] = jnp.exp(fric[...]) * work + smooth[:, :rows_y]

    sent = outgoing.at[:, pl.ds(0, ny - 1)]
    pltpu.make_async_copy(sent, sent, send_sem).wait()
    table_all = table_out.at[pl.ds(0, nx - 1)]
    pltpu.make_async_copy(table_all, table_all, table_send).wait()
    window_all = window_out.at[pl.ds(0, nx - 1)]
    pltpu.make_async_copy(window_all, window_all, window_send).wait()
    for side, there in ((0, "r"), (1, "l")):
        edges = pltpu.make_async_copy(edge_out.at[side], edge_out.at[side], edge_send.at[side])
        pl.when(has[there])(edges.wait)


def hand_on(adj_in, grad_in, adj_out, grad_out, sem):
    copies = [
        pltpu.make_async_copy(adj_in, adj_out, sem.at[0]), pltpu.make_async_copy(grad_in, grad_out, sem.at[1])
    ]
    for copy in copies:
        copy.start()
    for copy in copies:
        copy.wait()


def per_device(
    nx, ny, misfit, block_counts, slot_element, observe, stokes_blocks, pattern, velocity, log_friction
):
    _, peers, slots, width = misfit.shape
    rows_x, rows_y, offsets, blk, _ = stokes_blocks.shape
    elements = rows_x * rows_y
    lanes = 2 * blk
    half = slots // 2
    args = (
        misfit[0], block_counts, slot_element[0], observe.T, stokes_blocks,
        pattern.transpose(2, 0, 1), velocity, log_friction,
    )
    table = -(-2 * ny * half // (8 * lanes)) * 8
    vm, dma = pltpu.VMEM, pltpu.SemaphoreType.DMA
    made = pl.pallas_call(
        functools.partial(kernel, nx, ny),
        out_shape=(pltpu.VMEM((rows_x, rows_y, blk), F32), pltpu.VMEM((rows_x, rows_y), F32)),
        in_specs=[pl.BlockSpec(memory_space=pltpu.HBM)] * len(args),
        out_specs=(pl.BlockSpec(memory_space=pltpu.VMEM),) * 2,
        scratch_shapes=[vm(a.shape, a.dtype) for a in args]
        + [
            vm((nx, ny, half, lanes), BF16),
            vm((nx, ny, half, lanes), BF16),
            vm((peers, 128), F32),
            vm((nx, table, lanes), F32),
            vm((nx, table, lanes), F32),
            vm((nx, 2 * elements, ny * half), BF16),
            vm((offsets, rows_x, rows_y, lanes), BF16),
            vm(((nx * rows_x + 8 * 4) * rows_y, lanes), F32),
            vm((nx, (rows_x + 2) * rows_y // 2, lanes), BF16),
            vm((nx, (rows_x + 2) * rows_y // 2, lanes), BF16),
            vm((2, nx, 16, lanes), BF16),
            vm((2, nx, 16, lanes), BF16),
            vm((rows_x + 2, rows_y + 16, lanes), F32),
            vm((3, rows_x + 2, rows_y, lanes), BF16),
            vm((rows_x, 128), F32),
            vm((4, rows_x, 128), F32),
            dma((nx,)),
            dma((6,)),
            dma((rows_x,)),
            dma,
            dma((nx,)),
            dma,
            dma,
            dma((4,)),
            dma((4,)),
            dma,
            dma,
            dma((2,)),
            dma((2,)),
            pltpu.SemaphoreType.REGULAR,
            vm((rows_x, rows_y // 2, offsets, blk, lanes), BF16),
        ],
        compiler_params=pltpu.CompilerParams(
            collective_id=0, has_side_effects=True, vmem_limit_bytes=60 * 1024 * 1024
        ),
    )(*args)
    return pl.pallas_call(
        hand_on,
        out_shape=tuple(jax.ShapeDtypeStruct(a.shape, a.dtype) for a in made),
        in_specs=[pl.BlockSpec(memory_space=pltpu.VMEM)] * 2,
        out_specs=(pl.BlockSpec(memory_space=pltpu.HBM),) * 2,
        scratch_shapes=[pltpu.SemaphoreType.DMA((2,))],
        compiler_params=pltpu.CompilerParams(vmem_limit_bytes=1024 * 1024),
    )(*made)


def solution(mesh):
    in_specs = (
        P(("gx", "gy"), None, None, None),
        P(("gx", "gy"), None),
        P(("gx", "gy"), None, None),
        P(),
        P("gx", "gy", None, None, None),
        P("gx", "gy", None),
        P("gx", "gy", None),
        P("gx", "gy"),
    )
    out_specs = (P("gx", "gy", None), P("gx", "gy"))
    return jax.shard_map(
        functools.partial(per_device, mesh.shape["gx"], mesh.shape["gy"]),
        mesh=mesh, in_specs=in_specs, out_specs=out_specs, check_vma=False,
    )
```

```python
import functools

import jax
import jax.numpy as jnp
from jax import lax
from jax.experimental import pallas as pl
from jax.experimental.pallas import tpu as pltpu
from jax.sharding import PartitionSpec as P

MESH = pl.DeviceIdType.MESH
F32 = jnp.float32
BF16 = jnp.bfloat16


def iota(shape, dim):
    return lax.broadcasted_iota(jnp.int32, shape, dim)


def kernel(
    nx, ny,
    misfit_hbm, counts_hbm, elem_hbm, obs_hbm, stokes_hbm, pat_hbm, vel_hbm, fric_hbm,
    adj_ref, grad_ref,
    misfit, counts, elem, obs, stokes, pat, vel, fric,
    outgoing, arrived, placed, table_out, table_in, onehot, present, partial, window_out, window_in,
    edge_out, edge_in, cells, shifted, wide, near,
    misfit_sem, in_sem, stokes_sem, send_sem, recv_sem, table_send, table_recv, fric_send, fric_recv,
    window_send, window_recv, edge_send, edge_recv, vouch, packed,
):
    peers, slots, width = misfit.shape
    half = slots // 2
    rows_x, rows_y, offsets, blk, _ = stokes.shape
    elements = rows_x * rows_y
    lanes = 2 * blk
    reach = rows_x + 2
    gx, gy = lax.axis_index("gx"), lax.axis_index("gy")
    has = {"t": gx > 0, "b": gx < nx - 1, "l": gy > 0, "r": gy < ny - 1}

    high = (gx + nx - 1) // nx
    order = [(1 - high) * (nx - 1 - c) + high * c for c in range(nx)]

    misfit_loads = [
        pltpu.make_async_copy(
            misfit_hbm.at[pl.ds(order[c] * ny, ny)], misfit.at[pl.ds(order[c] * ny, ny)], misfit_sem.at[c]
        )
        for c in range(nx)
    ]
    loads = [
        pltpu.make_async_copy(src, dst, in_sem.at[n])
        for n, (src, dst) in enumerate(
            ((obs_hbm, obs), (elem_hbm, elem), (counts_hbm, counts), (fric_hbm, fric), (pat_hbm, pat), (vel_hbm, vel))
        )
    ]
    for load in loads[:1] + misfit_loads[:1] + loads[1:3] + misfit_loads[1:] + loads[3:]:
        load.start()

    for ref in (wide, near):
        ref[...] = jnp.zeros_like(ref)

    barrier = pltpu.get_barrier_semaphore()

    def greet(x, y):
        pl.semaphore_signal(barrier, inc=1, device_id=(x, y), device_id_type=MESH)

    for d in range(1, nx):
        greet(lax.rem(gx + d, nx), gy)
    for d in range(1, ny):
        greet(gx, lax.rem(gy + d, ny))

    stokes_loads = [
        pltpu.make_async_copy(stokes_hbm.at[x], stokes.at[x], stokes_sem.at[x]) for x in range(rows_x)
    ]
    for load in stokes_loads:
        load.start()

    partial[pl.ds(0, rows_y), :] = jnp.zeros((rows_y, lanes), F32)
    below = partial.shape[0] - (nx * rows_x + 1) * rows_y
    partial[pl.ds((nx * rows_x + 1) * rows_y, below), :] = jnp.zeros((below, lanes), F32)

    def no_edge(side):
        edge_in[side] = jnp.zeros_like(edge_in[side])

    pl.when(gy == 0)(functools.partial(no_edge, 0))
    pl.when(gy == ny - 1)(functools.partial(no_edge, 1))

    loads[1].wait()
    loads[2].wait()
    count = jnp.sum(
        jnp.where(iota((peers, peers), 0) == iota((peers, peers), 1), jnp.broadcast_to(counts[...], (peers, peers)), 0),
        axis=1, keepdims=True,
    )
    placed[:, :slots] = jnp.where(iota((peers, slots), 1) < count, elem[...], -1).astype(F32)
    per = lanes // half
    groups = peers // per
    own_groups = groups // nx
    rows = [jnp.zeros((groups, lanes), F32), jnp.zeros((groups, lanes), F32)]
    for j in range(per):
        part = placed[pl.ds(j, groups, stride=per), :][:, :slots].astype(BF16)
        for side in range(2):
            to = iota((slots, lanes), 0) - side * half
            place = (to >= 0) & (to < half) & (iota((slots, lanes), 1) == to + j * half)
            rows[side] = rows[side] + jnp.dot(
                part, jnp.where(place, 1.0, 0.0).astype(BF16), preferred_element_type=F32
            )
    table_out[...] = jnp.zeros_like(table_out)
    for i in range(nx):
        for side in range(2):
            table_out[i, side * own_groups : (side + 1) * own_groups, :] = rows[side][
                i * own_groups : (i + 1) * own_groups, :
            ]
    table_in[gx] = table_out[gx]

    loads[0].wait()
    zeros = jnp.zeros_like(obs[...])
    weights = jnp.concatenate(
        [jnp.concatenate([obs[...], zeros], axis=1), jnp.concatenate([zeros, obs[...]], axis=1)], axis=0
    )

    def project(c):
        misfit_loads[c].wait()
        first = order[c] * ny
        lo = misfit[pl.ds(first, ny), :half, :].reshape(ny * half, width)
        hi = misfit[pl.ds(first, ny), half:, :].reshape(ny * half, width)
        both = lax.dot_general(
            jnp.concatenate([lo, hi], axis=1), weights, (((1,), (1,)), ((), ())), preferred_element_type=F32
        )
        outgoing[order[c]] = both.astype(BF16).reshape(ny, half, lanes)

    project(0)

    loads[3].wait()
    wide[:, :rows_y] = fric[...]
    faces = [("t", 1, -1, 0), ("b", 0, 1, 0), ("l", 3, 0, -1), ("r", 2, 0, 1)]
    fric_copies = []
    for side, slot, dx, dy in faces:
        fric_copies.append(
            (
                side,
                pltpu.make_async_remote_copy(
                    src_ref=wide, dst_ref=near.at[slot], send_sem=fric_send.at[slot], recv_sem=fric_recv.at[slot],
                    device_id=(gx + dx, gy + dy), device_id_type=MESH,
                ),
            )
        )
    pl.semaphore_wait(barrier, nx + ny - 2)
    for d in range(1, nx):
        pl.semaphore_signal(vouch, inc=1, device_id=(lax.rem(gx + d, nx), gy), device_id_type=MESH)
    for d in range(1, nx):
        other = lax.rem(gx + d, nx)
        pltpu.make_async_remote_copy(
            src_ref=table_out.at[other], dst_ref=table_in.at[gx], send_sem=table_send, recv_sem=table_recv,
            device_id=(other, gy), device_id_type=MESH,
        ).start()

    for c in range(nx):
        if c > 0:
            project(c)

        def send(d, carry, c=c):
            peer = lax.rem(gy + d, ny)
            pltpu.make_async_remote_copy(
                src_ref=outgoing.at[order[c], peer], dst_ref=arrived.at[order[c], gy],
                send_sem=send_sem, recv_sem=recv_sem.at[c], device_id=(gx, peer), device_id_type=MESH,
            ).start()
            return carry

        lax.fori_loop(1, ny, send, 0)

    for side, copy in fric_copies:
        pl.when(has[side])(copy.start)

    for c in range(nx):
        arrived[order[c], gy] = outgoing[order[c], gy]

    def pack(first, last):
        for x in range(first, last):
            stokes_loads[x].wait()
            packed[x] = jnp.concatenate([stokes[x, : rows_y // 2], stokes[x, rows_y // 2 :]], axis=-1)

    pack(0, 5)

    table_all = table_in.at[pl.ds(0, nx - 1)]
    pltpu.make_async_copy(table_all, table_all, table_recv).wait()
    which = iota((elements, lanes), 0).astype(F32)
    for i in range(nx):
        for side in range(2):
            for g in range(own_groups):
                row = jnp.broadcast_to(table_in[i, side * own_groups + g : side * own_groups + g + 1, :], (elements, lanes))
                onehot[i, side * elements : (side + 1) * elements, g * lanes : (g + 1) * lanes] = jnp.where(
                    which == row, 1.0, 0.0
                ).astype(BF16)

    pl.semaphore_wait(vouch, nx - 1)
    left_lanes = iota((elements, lanes), 1) < blk
    span = reach * rows_y // 2
    window_lanes = iota((span, lanes), 1) < blk

    def pass_on(to):
        first = to * elements
        one = partial[pl.ds(first, span), :]
        two = partial[pl.ds(first + span, span), :]
        window = jnp.where(window_lanes, one, two).astype(BF16)

        def keep():
            window_in[gx] = window

        def give():
            window_out[to] = window
            pltpu.make_async_remote_copy(
                src_ref=window_out.at[to], dst_ref=window_in.at[gx], send_sem=window_send, recv_sem=window_recv,
                device_id=(to, gy), device_id_type=MESH,
            ).start()

        pl.when(to == gx)(keep)
        pl.when(to != gx)(give)
        for side, there, dy, column in ((0, "r", 1, rows_y - 1), (1, "l", -1, 0)):
            edge_out[side, to] = partial[pl.ds(first + column, 16, stride=rows_y), :].astype(BF16)

            def give_edge(side=side, dy=dy):
                pltpu.make_async_remote_copy(
                    src_ref=edge_out.at[side, to], dst_ref=edge_in.at[side, gx],
                    send_sem=edge_send.at[side], recv_sem=edge_recv.at[side],
                    device_id=(to, gy + dy), device_id_type=MESH,
                ).start()

            pl.when(has[there])(give_edge)

    for c in range(nx):
        now = order[c]
        landed = arrived.at[now, pl.ds(0, ny - 1)]
        pltpu.make_async_copy(landed, landed, recv_sem.at[c]).wait()
        sums = jnp.dot(
            onehot[now], arrived[now].reshape(ny * half, lanes), preferred_element_type=F32
        )
        mixed = jnp.where(left_lanes, sums[:elements], sums[elements:])
        partial[pl.ds(rows_y + now * elements, elements), :] = mixed + pltpu.roll(mixed, blk, axis=1)
        if c > 0:
            pass_on(order[c - 1])
    pass_on(order[nx - 1])

    loads[4].wait()
    eye = jnp.where(iota((rows_y, rows_y), 0) == iota((rows_y, rows_y), 1), 1.0, 0.0)
    tags = pat[...].astype(F32).reshape(offsets * rows_x, rows_y)
    tags = jnp.broadcast_to(tags[:, None, :], (offsets * rows_x, rows_y, rows_y)) * eye[None]
    spread = jnp.dot(
        tags.reshape(offsets * elements, rows_y).astype(BF16), jnp.ones((rows_y, lanes), BF16),
        preferred_element_type=F32,
    )
    present[...] = spread.astype(BF16).reshape(offsets, rows_x, rows_y, lanes)
    pack(5, rows_x)

    window_all = window_in.at[pl.ds(0, nx - 1)]
    pltpu.make_async_copy(window_all, window_all, window_recv).wait()
    total = window_in[0].astype(F32)
    for i in range(1, nx):
        total = total + window_in[i].astype(F32)
    turned = pltpu.roll(total, blk, axis=1)
    for part, rows_of in enumerate((jnp.where(window_lanes, total, turned), jnp.where(window_lanes, turned, total))):
        for r in range(reach // 2):
            cells[part * (reach // 2) + r, 8 : 8 + rows_y] = rows_of[r * rows_y : (r + 1) * rows_y]
    for side, there, at in ((0, "l", 7), (1, "r", 8 + rows_y)):
        edges = pltpu.make_async_copy(edge_in.at[side], edge_in.at[side], edge_recv.at[side])
        pl.when(has[there])(edges.wait)
        edge = edge_in[side, 0].astype(F32)
        for i in range(1, nx):
            edge = edge + edge_in[side, i].astype(F32)
        for r in range(reach):
            cells[r, at : at + 1, :] = edge[r : r + 1, :]
    for q in (-1, 0, 1):
        for r in range(reach):
            shifted[q + 1, r] = cells[r, 8 - q : 8 - q + rows_y, :].astype(BF16)

    lane_block = iota((rows_y, lanes), 1) // blk
    row_of = iota((rows_y, lanes), 0)
    masks = [
        jnp.where(lax.rem(row_of, rows_y // 2) == 2 * c + lane_block, 1.0, 0.0).astype(BF16)
        for c in range(rows_y // 4)
    ]

    def row(x, carry):
        total = jnp.zeros((rows_y, lanes), F32)
        for k in range(9):
            p, q = k // 3 - 1, k % 3 - 1
            source = shifted[q + 1, 1 + x - p] * present[k, x]
            left = jnp.concatenate([source * mask for mask in masks], axis=1)
            right = packed[x, :, k].reshape(rows_y // 2 * blk, lanes)
            total = total + jnp.dot(left, right, preferred_element_type=F32)
        adj_ref[x] = jnp.where(row_of < rows_y // 2, total, pltpu.roll(total, blk, axis=1))[:, :blk]
        return carry

    lax.fori_loop(0, rows_x, row, 0, unroll=8)

    loads[5].wait()
    for side, copy in fric_copies:
        pl.when(has[side])(copy.wait_send)
    for side, slot, dx, dy in faces:
        back = [c for c in fric_copies if c[0] == {"t": "b", "b": "t", "l": "r", "r": "l"}[side]][0][1]
        pl.when(has[side])(back.wait_recv)
    level = wide[...]
    row_id, lane_id = iota(level.shape, 0), iota(level.shape, 1)
    above = jnp.where(row_id == 0, pltpu.roll(near[0], 1, axis=0), pltpu.roll(level, 1, axis=0))
    below = jnp.where(
        row_id == rows_x - 1, pltpu.roll(near[1], rows_x - 1, axis=0), pltpu.roll(level, rows_x - 1, axis=0)
    )
    width_f = level.shape[1]
    before = jnp.where(
        lane_id == 0, pltpu.roll(near[2], width_f - rows_y + 1, axis=1), pltpu.roll(level, 1, axis=1)
    )
    after = jnp.where(
        lane_id == rows_y - 1, pltpu.roll(near[3], rows_y - 1, axis=1), pltpu.roll(level, width_f - 1, axis=1)
    )
    smooth = 0.5 * (4.0 * level - (above + below + before + after))
    work = []
    for x in range(rows_x):
        column = jnp.sum(vel[x].astype(F32) * adj_ref[x], axis=1, keepdims=True)
        work.append(jnp.sum(jnp.broadcast_to(column, (rows_y, rows_y)) * eye, axis=0, keepdims=True))
    work = jnp.concatenate(work, axis=0)
    grad_ref[...] = jnp.exp(fric[...]) * work + smooth[:, :rows_y]

    sent = outgoing.at[:, pl.ds(0, ny - 1)]
    pltpu.make_async_copy(sent, sent, send_sem).wait()
    table_all = table_out.at[pl.ds(0, nx - 1)]
    pltpu.make_async_copy(table_all, table_all, table_send).wait()
    window_all = window_out.at[pl.ds(0, nx - 1)]
    pltpu.make_async_copy(window_all, window_all, window_send).wait()
    for side, there in ((0, "r"), (1, "l")):
        edges = pltpu.make_async_copy(edge_out.at[side], edge_out.at[side], edge_send.at[side])
        pl.when(has[there])(edges.wait)


def hand_on(adj_in, grad_in, adj_out, grad_out, sem):
    copies = [
        pltpu.make_async_copy(adj_in, adj_out, sem.at[0]), pltpu.make_async_copy(grad_in, grad_out, sem.at[1])
    ]
    for copy in copies:
        copy.start()
    for copy in copies:
        copy.wait()


def per_device(
    nx, ny, misfit, block_counts, slot_element, observe, stokes_blocks, pattern, velocity, log_friction
):
    _, peers, slots, width = misfit.shape
    rows_x, rows_y, offsets, blk, _ = stokes_blocks.shape
    elements = rows_x * rows_y
    lanes = 2 * blk
    half = slots // 2
    args = (
        misfit[0], block_counts, slot_element[0], observe.T, stokes_blocks,
        pattern.transpose(2, 0, 1), velocity, log_friction,
    )
    table = -(-2 * ny * half // (8 * lanes)) * 8
    vm, dma = pltpu.VMEM, pltpu.SemaphoreType.DMA
    made = pl.pallas_call(
        functools.partial(kernel, nx, ny),
        out_shape=(pltpu.VMEM((rows_x, rows_y, blk), F32), pltpu.VMEM((rows_x, rows_y), F32)),
        in_specs=[pl.BlockSpec(memory_space=pltpu.HBM)] * len(args),
        out_specs=(pl.BlockSpec(memory_space=pltpu.VMEM),) * 2,
        scratch_shapes=[vm(a.shape, a.dtype) for a in args]
        + [
            vm((nx, ny, half, lanes), BF16),
            vm((nx, ny, half, lanes), BF16),
            vm((peers, 128), F32),
            vm((nx, table, lanes), F32),
            vm((nx, table, lanes), F32),
            vm((nx, 2 * elements, ny * half), BF16),
            vm((offsets, rows_x, rows_y, lanes), BF16),
            vm(((nx * rows_x + 8 * 4) * rows_y, lanes), F32),
            vm((nx, (rows_x + 2) * rows_y // 2, lanes), BF16),
            vm((nx, (rows_x + 2) * rows_y // 2, lanes), BF16),
            vm((2, nx, 16, lanes), BF16),
            vm((2, nx, 16, lanes), BF16),
            vm((rows_x + 2, rows_y + 16, lanes), F32),
            vm((3, rows_x + 2, rows_y, lanes), BF16),
            vm((rows_x, 128), F32),
            vm((4, rows_x, 128), F32),
            dma((nx,)),
            dma((6,)),
            dma((rows_x,)),
            dma,
            dma((nx,)),
            dma,
            dma,
            dma((4,)),
            dma((4,)),
            dma,
            dma,
            dma((2,)),
            dma((2,)),
            pltpu.SemaphoreType.REGULAR,
            vm((rows_x, rows_y // 2, offsets, blk, lanes), BF16),
        ],
        compiler_params=pltpu.CompilerParams(
            collective_id=0, has_side_effects=True, vmem_limit_bytes=60 * 1024 * 1024
        ),
    )(*args)
    return pl.pallas_call(
        hand_on,
        out_shape=tuple(jax.ShapeDtypeStruct(a.shape, a.dtype) for a in made),
        in_specs=[pl.BlockSpec(memory_space=pltpu.VMEM)] * 2,
        out_specs=(pl.BlockSpec(memory_space=pltpu.HBM),) * 2,
        scratch_shapes=[pltpu.SemaphoreType.DMA((2,))],
        compiler_params=pltpu.CompilerParams(vmem_limit_bytes=1024 * 1024),
    )(*made)


def solution(mesh):
    in_specs = (
        P(("gx", "gy"), None, None, None),
        P(("gx", "gy"), None),
        P(("gx", "gy"), None, None),
        P(),
        P("gx", "gy", None, None, None),
        P("gx", "gy", None),
        P("gx", "gy", None),
        P("gx", "gy"),
    )
    out_specs = (P("gx", "gy", None), P("gx", "gy"))
    return jax.shard_map(
        functools.partial(per_device, mesh.shape["gx"], mesh.shape["gy"]),
        mesh=mesh, in_specs=in_specs, out_specs=out_specs, check_vma=False,
    )
```

```python
import functools

import jax
import jax.numpy as jnp
from jax import lax
from jax.experimental import pallas as pl
from jax.experimental.pallas import tpu as pltpu
from jax.sharding import PartitionSpec as P

MESH = pl.DeviceIdType.MESH
F32 = jnp.float32
BF16 = jnp.bfloat16


def iota(shape, dim):
    return lax.broadcasted_iota(jnp.int32, shape, dim)


def kernel(
    nx, ny,
    misfit_hbm, counts_hbm, elem_hbm, obs_hbm, stokes_hbm, pat_hbm, vel_hbm, fric_hbm,
    adj_ref, grad_ref,
    misfit, counts, elem, obs, stokes, pat, vel, fric,
    outgoing, arrived, placed, table_out, table_in, onehot, present, partial, window_out, window_in,
    edge_out, edge_in, cells, shifted, wide, near,
    misfit_sem, in_sem, stokes_sem, send_sem, recv_sem, table_send, table_recv, fric_send, fric_recv,
    window_send, window_recv, edge_send, edge_recv, vouch, packed,
):
    peers, slots, width = misfit.shape
    half = slots // 2
    rows_x, rows_y, offsets, blk, _ = stokes.shape
    elements = rows_x * rows_y
    lanes = 2 * blk
    reach = rows_x + 2
    gx, gy = lax.axis_index("gx"), lax.axis_index("gy")
    has = {"t": gx > 0, "b": gx < nx - 1, "l": gy > 0, "r": gy < ny - 1}

    high = (gx + nx - 1) // nx
    order = [(1 - high) * (nx - 1 - c) + high * c for c in range(nx)]

    misfit_loads = [
        pltpu.make_async_copy(
            misfit_hbm.at[pl.ds(order[c] * ny, ny)], misfit.at[pl.ds(order[c] * ny, ny)], misfit_sem.at[c]
        )
        for c in range(nx)
    ]
    loads = [
        pltpu.make_async_copy(src, dst, in_sem.at[n])
        for n, (src, dst) in enumerate(
            ((obs_hbm, obs), (elem_hbm, elem), (counts_hbm, counts), (fric_hbm, fric), (pat_hbm, pat), (vel_hbm, vel))
        )
    ]
    for load in loads[:1] + misfit_loads[:1] + loads[1:3] + misfit_loads[1:] + loads[3:]:
        load.start()

    for ref in (wide, near):
        ref[...] = jnp.zeros_like(ref)

    barrier = pltpu.get_barrier_semaphore()

    def greet(x, y):
        pl.semaphore_signal(barrier, inc=1, device_id=(x, y), device_id_type=MESH)

    for d in range(1, nx):
        greet(lax.rem(gx + d, nx), gy)
    for d in range(1, ny):
        greet(gx, lax.rem(gy + d, ny))

    stokes_loads = [
        pltpu.make_async_copy(stokes_hbm.at[x], stokes.at[x], stokes_sem.at[x]) for x in range(rows_x)
    ]
    for load in stokes_loads:
        load.start()

    partial[pl.ds(0, rows_y), :] = jnp.zeros((rows_y, lanes), F32)
    below = partial.shape[0] - (nx * rows_x + 1) * rows_y
    partial[pl.ds((nx * rows_x + 1) * rows_y, below), :] = jnp.zeros((below, lanes), F32)

    def no_edge(side):
        edge_in[side] = jnp.zeros_like(edge_in[side])

    pl.when(gy == 0)(functools.partial(no_edge, 0))
    pl.when(gy == ny - 1)(functools.partial(no_edge, 1))

    loads[1].wait()
    loads[2].wait()
    count = jnp.sum(
        jnp.where(iota((peers, peers), 0) == iota((peers, peers), 1), jnp.broadcast_to(counts[...], (peers, peers)), 0),
        axis=1, keepdims=True,
    )
    placed[:, :slots] = jnp.where(iota((peers, slots), 1) < count, elem[...], -1).astype(F32)
    per = lanes // half
    groups = peers // per
    own_groups = groups // nx
    rows = [jnp.zeros((groups, lanes), F32), jnp.zeros((groups, lanes), F32)]
    for j in range(per):
        part = placed[pl.ds(j, groups, stride=per), :][:, :slots].astype(BF16)
        for side in range(2):
            to = iota((slots, lanes), 0) - side * half
            place = (to >= 0) & (to < half) & (iota((slots, lanes), 1) == to + j * half)
            rows[side] = rows[side] + jnp.dot(
                part, jnp.where(place, 1.0, 0.0).astype(BF16), preferred_element_type=F32
            )
    table_out[...] = jnp.zeros_like(table_out)
    for i in range(nx):
        for side in range(2):
            table_out[i, side * own_groups : (side + 1) * own_groups, :] = rows[side][
                i * own_groups : (i + 1) * own_groups, :
            ]
    table_in[gx] = table_out[gx]

    loads[0].wait()
    zeros = jnp.zeros_like(obs[...])
    weights = jnp.concatenate(
        [jnp.concatenate([obs[...], zeros], axis=1), jnp.concatenate([zeros, obs[...]], axis=1)], axis=0
    )

    def project(c):
        misfit_loads[c].wait()
        first = order[c] * ny
        lo = misfit[pl.ds(first, ny), :half, :].reshape(ny * half, width)
        hi = misfit[pl.ds(first, ny), half:, :].reshape(ny * half, width)
        both = lax.dot_general(
            jnp.concatenate([lo, hi], axis=1), weights, (((1,), (1,)), ((), ())), preferred_element_type=F32
        )
        outgoing[order[c]] = both.astype(BF16).reshape(ny, half, lanes)

    project(0)

    loads[3].wait()
    wide[:, :rows_y] = fric[...]
    faces = [("t", 1, -1, 0), ("b", 0, 1, 0), ("l", 3, 0, -1), ("r", 2, 0, 1)]
    fric_copies = []
    for side, slot, dx, dy in faces:
        fric_copies.append(
            (
                side,
                pltpu.make_async_remote_copy(
                    src_ref=wide, dst_ref=near.at[slot], send_sem=fric_send.at[slot], recv_sem=fric_recv.at[slot],
                    device_id=(gx + dx, gy + dy), device_id_type=MESH,
                ),
            )
        )
    pl.semaphore_wait(barrier, nx + ny - 2)
    for d in range(1, nx):
        pl.semaphore_signal(vouch, inc=1, device_id=(lax.rem(gx + d, nx), gy), device_id_type=MESH)
    for d in range(1, nx):
        other = lax.rem(gx + d, nx)
        pltpu.make_async_remote_copy(
            src_ref=table_out.at[other], dst_ref=table_in.at[gx], send_sem=table_send, recv_sem=table_recv,
            device_id=(other, gy), device_id_type=MESH,
        ).start()

    for c in range(nx):
        if c > 0:
            project(c)

        def send(d, carry, c=c):
            peer = lax.rem(gy + d, ny)
            pltpu.make_async_remote_copy(
                src_ref=outgoing.at[order[c], peer], dst_ref=arrived.at[order[c], gy],
                send_sem=send_sem, recv_sem=recv_sem.at[c], device_id=(gx, peer), device_id_type=MESH,
            ).start()
            return carry

        lax.fori_loop(1, ny, send, 0)

    for side, copy in fric_copies:
        pl.when(has[side])(copy.start)

    for c in range(nx):
        arrived[order[c], gy] = outgoing[order[c], gy]

    def pack(first, last):
        for x in range(first, last):
            stokes_loads[x].wait()
            packed[x] = jnp.concatenate([stokes[x, : rows_y // 2], stokes[x, rows_y // 2 :]], axis=-1)

    pack(0, 5)

    table_all = table_in.at[pl.ds(0, nx - 1)]
    pltpu.make_async_copy(table_all, table_all, table_recv).wait()
    which = iota((elements, lanes), 0).astype(F32)
    for i in range(nx):
        for side in range(2):
            for g in range(own_groups):
                row = jnp.broadcast_to(table_in[i, side * own_groups + g : side * own_groups + g + 1, :], (elements, lanes))
                onehot[i, side * elements : (side + 1) * elements, g * lanes : (g + 1) * lanes] = jnp.where(
                    which == row, 1.0, 0.0
                ).astype(BF16)

    pl.semaphore_wait(vouch, nx - 1)
    left_lanes = iota((elements, lanes), 1) < blk
    span = reach * rows_y // 2
    window_lanes = iota((span, lanes), 1) < blk

    def pass_on(to):
        first = to * elements
        one = partial[pl.ds(first, span), :]
        two = partial[pl.ds(first + span, span), :]
        window = jnp.where(window_lanes, one, two).astype(BF16)

        def keep():
            window_in[gx] = window

        def give():
            window_out[to] = window
            pltpu.make_async_remote_copy(
                src_ref=window_out.at[to], dst_ref=window_in.at[gx], send_sem=window_send, recv_sem=window_recv,
                device_id=(to, gy), device_id_type=MESH,
            ).start()

        pl.when(to == gx)(keep)
        away = to != gx
        pl.when(jnp.logical_and(away, gy == 0))(give)
        for side, there, dy, column in ((0, "r", 1, rows_y - 1), (1, "l", -1, 0)):
            edge_out[side, to] = partial[pl.ds(first + column, 16, stride=rows_y), :].astype(BF16)

            def give_edge(side=side, dy=dy):
                pltpu.make_async_remote_copy(
                    src_ref=edge_out.at[side, to], dst_ref=edge_in.at[side, gx],
                    send_sem=edge_send.at[side], recv_sem=edge_recv.at[side],
                    device_id=(to, gy + dy), device_id_type=MESH,
                ).start()

            pl.when(has[there])(give_edge)
        pl.when(jnp.logical_and(away, gy > 0))(give)

    for c in range(nx):
        now = order[c]
        landed = arrived.at[now, pl.ds(0, ny - 1)]
        pltpu.make_async_copy(landed, landed, recv_sem.at[c]).wait()
        sums = jnp.dot(
            onehot[now], arrived[now].reshape(ny * half, lanes), preferred_element_type=F32
        )
        mixed = jnp.where(left_lanes, sums[:elements], sums[elements:])
        partial[pl.ds(rows_y + now * elements, elements), :] = mixed + pltpu.roll(mixed, blk, axis=1)
        if c > 0:
            pass_on(order[c - 1])
    pass_on(order[nx - 1])

    loads[4].wait()
    eye = jnp.where(iota((rows_y, rows_y), 0) == iota((rows_y, rows_y), 1), 1.0, 0.0)
    tags = pat[...].astype(F32).reshape(offsets * rows_x, rows_y)
    tags = jnp.broadcast_to(tags[:, None, :], (offsets * rows_x, rows_y, rows_y)) * eye[None]
    spread = jnp.dot(
        tags.reshape(offsets * elements, rows_y).astype(BF16), jnp.ones((rows_y, lanes), BF16),
        preferred_element_type=F32,
    )
    present[...] = spread.astype(BF16).reshape(offsets, rows_x, rows_y, lanes)
    pack(5, rows_x)

    window_all = window_in.at[pl.ds(0, nx - 1)]
    pltpu.make_async_copy(window_all, window_all, window_recv).wait()
    total = window_in[0].astype(F32)
    for i in range(1, nx):
        total = total + window_in[i].astype(F32)
    turned = pltpu.roll(total, blk, axis=1)
    for part, rows_of in enumerate((jnp.where(window_lanes, total, turned), jnp.where(window_lanes, turned, total))):
        for r in range(reach // 2):
            cells[part * (reach // 2) + r, 8 : 8 + rows_y] = rows_of[r * rows_y : (r + 1) * rows_y]
    for side, there, at in ((0, "l", 7), (1, "r", 8 + rows_y)):
        edges = pltpu.make_async_copy(edge_in.at[side], edge_in.at[side], edge_recv.at[side])
        pl.when(has[there])(edges.wait)
        edge = edge_in[side, 0].astype(F32)
        for i in range(1, nx):
            edge = edge + edge_in[side, i].astype(F32)
        for r in range(reach):
            cells[r, at : at + 1, :] = edge[r : r + 1, :]
    for q in (-1, 0, 1):
        for r in range(reach):
            shifted[q + 1, r] = cells[r, 8 - q : 8 - q + rows_y, :].astype(BF16)

    lane_block = iota((rows_y, lanes), 1) // blk
    row_of = iota((rows_y, lanes), 0)
    masks = [
        jnp.where(lax.rem(row_of, rows_y // 2) == 2 * c + lane_block, 1.0, 0.0).astype(BF16)
        for c in range(rows_y // 4)
    ]

    def row(x, carry):
        total = jnp.zeros((rows_y, lanes), F32)
        for k in range(9):
            p, q = k // 3 - 1, k % 3 - 1
            source = shifted[q + 1, 1 + x - p] * present[k, x]
            left = jnp.concatenate([source * mask for mask in masks], axis=1)
            right = packed[x, :, k].reshape(rows_y // 2 * blk, lanes)
            total = total + jnp.dot(left, right, preferred_element_type=F32)
        adj_ref[x] = jnp.where(row_of < rows_y // 2, total, pltpu.roll(total, blk, axis=1))[:, :blk]
        return carry

    lax.fori_loop(0, rows_x, row, 0, unroll=8)

    loads[5].wait()
    for side, copy in fric_copies:
        pl.when(has[side])(copy.wait_send)
    for side, slot, dx, dy in faces:
        back = [c for c in fric_copies if c[0] == {"t": "b", "b": "t", "l": "r", "r": "l"}[side]][0][1]
        pl.when(has[side])(back.wait_recv)
    level = wide[...]
    row_id, lane_id = iota(level.shape, 0), iota(level.shape, 1)
    above = jnp.where(row_id == 0, pltpu.roll(near[0], 1, axis=0), pltpu.roll(level, 1, axis=0))
    below = jnp.where(
        row_id == rows_x - 1, pltpu.roll(near[1], rows_x - 1, axis=0), pltpu.roll(level, rows_x - 1, axis=0)
    )
    width_f = level.shape[1]
    before = jnp.where(
        lane_id == 0, pltpu.roll(near[2], width_f - rows_y + 1, axis=1), pltpu.roll(level, 1, axis=1)
    )
    after = jnp.where(
        lane_id == rows_y - 1, pltpu.roll(near[3], rows_y - 1, axis=1), pltpu.roll(level, width_f - 1, axis=1)
    )
    smooth = 0.5 * (4.0 * level - (above + below + before + after))
    work = []
    for x in range(rows_x):
        column = jnp.sum(vel[x].astype(F32) * adj_ref[x], axis=1, keepdims=True)
        work.append(jnp.sum(jnp.broadcast_to(column, (rows_y, rows_y)) * eye, axis=0, keepdims=True))
    work = jnp.concatenate(work, axis=0)
    grad_ref[...] = jnp.exp(fric[...]) * work + smooth[:, :rows_y]

    sent = outgoing.at[:, pl.ds(0, ny - 1)]
    pltpu.make_async_copy(sent, sent, send_sem).wait()
    table_all = table_out.at[pl.ds(0, nx - 1)]
    pltpu.make_async_copy(table_all, table_all, table_send).wait()
    window_all = window_out.at[pl.ds(0, nx - 1)]
    pltpu.make_async_copy(window_all, window_all, window_send).wait()
    for side, there in ((0, "r"), (1, "l")):
        edges = pltpu.make_async_copy(edge_out.at[side], edge_out.at[side], edge_send.at[side])
        pl.when(has[there])(edges.wait)


def hand_on(adj_in, grad_in, adj_out, grad_out, sem):
    copies = [
        pltpu.make_async_copy(adj_in, adj_out, sem.at[0]), pltpu.make_async_copy(grad_in, grad_out, sem.at[1])
    ]
    for copy in copies:
        copy.start()
    for copy in copies:
        copy.wait()


def per_device(
    nx, ny, misfit, block_counts, slot_element, observe, stokes_blocks, pattern, velocity, log_friction
):
    _, peers, slots, width = misfit.shape
    rows_x, rows_y, offsets, blk, _ = stokes_blocks.shape
    elements = rows_x * rows_y
    lanes = 2 * blk
    half = slots // 2
    args = (
        misfit[0], block_counts, slot_element[0], observe.T, stokes_blocks,
        pattern.transpose(2, 0, 1), velocity, log_friction,
    )
    table = -(-2 * ny * half // (8 * lanes)) * 8
    vm, dma = pltpu.VMEM, pltpu.SemaphoreType.DMA
    made = pl.pallas_call(
        functools.partial(kernel, nx, ny),
        out_shape=(pltpu.VMEM((rows_x, rows_y, blk), F32), pltpu.VMEM((rows_x, rows_y), F32)),
        in_specs=[pl.BlockSpec(memory_space=pltpu.HBM)] * len(args),
        out_specs=(pl.BlockSpec(memory_space=pltpu.VMEM),) * 2,
        scratch_shapes=[vm(a.shape, a.dtype) for a in args]
        + [
            vm((nx, ny, half, lanes), BF16),
            vm((nx, ny, half, lanes), BF16),
            vm((peers, 128), F32),
            vm((nx, table, lanes), F32),
            vm((nx, table, lanes), F32),
            vm((nx, 2 * elements, ny * half), BF16),
            vm((offsets, rows_x, rows_y, lanes), BF16),
            vm(((nx * rows_x + 8 * 4) * rows_y, lanes), F32),
            vm((nx, (rows_x + 2) * rows_y // 2, lanes), BF16),
            vm((nx, (rows_x + 2) * rows_y // 2, lanes), BF16),
            vm((2, nx, 16, lanes), BF16),
            vm((2, nx, 16, lanes), BF16),
            vm((rows_x + 2, rows_y + 16, lanes), F32),
            vm((3, rows_x + 2, rows_y, lanes), BF16),
            vm((rows_x, 128), F32),
            vm((4, rows_x, 128), F32),
            dma((nx,)),
            dma((6,)),
            dma((rows_x,)),
            dma,
            dma((nx,)),
            dma,
            dma,
            dma((4,)),
            dma((4,)),
            dma,
            dma,
            dma((2,)),
            dma((2,)),
            pltpu.SemaphoreType.REGULAR,
            vm((rows_x, rows_y // 2, offsets, blk, lanes), BF16),
        ],
        compiler_params=pltpu.CompilerParams(
            collective_id=0, has_side_effects=True, vmem_limit_bytes=60 * 1024 * 1024
        ),
    )(*args)
    return pl.pallas_call(
        hand_on,
        out_shape=tuple(jax.ShapeDtypeStruct(a.shape, a.dtype) for a in made),
        in_specs=[pl.BlockSpec(memory_space=pltpu.VMEM)] * 2,
        out_specs=(pl.BlockSpec(memory_space=pltpu.HBM),) * 2,
        scratch_shapes=[pltpu.SemaphoreType.DMA((2,))],
        compiler_params=pltpu.CompilerParams(vmem_limit_bytes=1024 * 1024),
    )(*made)


def solution(mesh):
    in_specs = (
        P(("gx", "gy"), None, None, None),
        P(("gx", "gy"), None),
        P(("gx", "gy"), None, None),
        P(),
        P("gx", "gy", None, None, None),
        P("gx", "gy", None),
        P("gx", "gy", None),
        P("gx", "gy"),
    )
    out_specs = (P("gx", "gy", None), P("gx", "gy"))
    return jax.shard_map(
        functools.partial(per_device, mesh.shape["gx"], mesh.shape["gy"]),
        mesh=mesh, in_specs=in_specs, out_specs=out_specs, check_vma=False,
    )
```
